32 devices in a mesh: ens: 2 (over y), band: 4 (over z), feat: 2 (over x), sub: 2 (over core).
Axes of the slice: x: 2, y: 2, z: 4, core: 2. Of those that a mesh axis runs over, the one named last changes fastest.
Arguments:
- grid_state: bfloat16 [16384, 512], P(('ens', 'band', 'feat', 'sub')), parts along dimension 0, may hold values from -6 to 6
- mesh_state: bfloat16 [16384, 512], P(('ens', 'band', 'feat', 'sub')), parts along dimension 0, may hold values from -6 to 6
- g2m_sender: int32 [16384], P(('band', 'feat', 'sub')), may hold values from 0 to 511
- g2m_slot: int32 [16384], P(('band', 'feat', 'sub')), may hold values from 0 to 383, as said below
- g2m_land: int32 [6144], P(('band', 'feat', 'sub')), may hold values from 0 to 511
- mesh_sender: int32 [32768], P(('band', 'feat', 'sub')), may hold values from 0 to 767
- mesh_receiver: int32 [32768], P(('band', 'feat', 'sub')), may hold values from 0 to 511
- m2g_sender: int32 [24576], P(('band', 'feat', 'sub')), may hold values from 0 to 767
- m2g_receiver: int32 [24576], P(('band', 'feat', 'sub')), may hold values from 0 to 511
- enc_msg_w1: bfloat16 [512, 512], P('band'), may hold values from -0.25 to 0.25
- enc_msg_b1: float32 [512], replicated, may hold values from -3 to 3
- enc_msg_w2: bfloat16 [512, 512], P('band'), may hold values from -0.25 to 0.25
- enc_node_w1: bfloat16 [1024, 512], P('band'), may hold values from -0.1875 to 0.1875
- enc_node_b1: float32 [512], replicated, may hold values from -3 to 3
- enc_node_w2: bfloat16 [512, 512], P('band'), may hold values from -0.25 to 0.25
- enc_gain: float32 [512], replicated, may hold values from 0.1 to 1.9
- proc_msg_w1: bfloat16 [1, 1024, 512], P(None, 'band'), may hold values from -0.1875 to 0.1875
- proc_msg_b1: float32 [1, 512], replicated, may hold values from -3 to 3
- proc_msg_w2: bfloat16 [1, 512, 512], P(None, 'band'), may hold values from -0.25 to 0.25
- proc_node_w1: bfloat16 [1, 1024, 512], P(None, 'band'), may hold values from -0.1875 to 0.1875
- proc_node_b1: float32 [1, 512], replicated, may hold values from -3 to 3
- proc_node_w2: bfloat16 [1, 512, 512], P(None, 'band'), may hold values from -0.25 to 0.25
- proc_gain: float32 [1, 512], replicated, may hold values from 0.1 to 1.9
- dec_msg_w1: bfloat16 [1024, 512], P('band'), may hold values from -0.1875 to 0.1875
- dec_msg_b1: float32 [512], replicated, may hold values from -3 to 3
- dec_msg_w2: bfloat16 [512, 512], P('band'), may hold values from -0.25 to 0.25
- dec_node_w1: bfloat16 [1024, 512], P('band'), may hold values from -0.1875 to 0.1875
- dec_node_b1: float32 [512], replicated, may hold values from -3 to 3
- dec_node_w2: bfloat16 [512, 512], P('band'), may hold values from -0.25 to 0.25
- dec_gain: float32 [512], replicated, may hold values from 0.1 to 1.9
Outputs:
- grid_next: bfloat16 [16384, 512], P(('ens', 'band', 'feat', 'sub')), parts along dimension 0
The draws below stay inside these ranges and needn't reach their ends.
There are 2 independent parts, one for each index of `ens`. The reference program is written for one: setup_inputs(seed, part) draws one part's arguments, and reference() takes and returns one part's arrays. A program takes and returns all parts, laid end to end along the dimension named above; an argument that names none is the same for every part. Nothing has to cross between parts.
Inputs may be any that keep to these rules, and one draw needn't show every extreme that they name: `g2m_sender`: A grid row among the 512 rows of the edge's own device. `g2m_slot`: slot k * 128 + c of a device (k = 0, 1, 2) goes to the device k - 1 places further along band+feat+sub. The first device uses no slot with k = 0 and the last none with k = 2; every other slot of a device is used by one edge or more. `g2m_land`: entry k * 128 + c of a device's block: its own mesh row where slot k * 128 + c of the device k - 1 places before it lands. `mesh_sender`: A row of the device's extended mesh rows: the previous device's last 128 mesh rows, its own 512, the next device's first 128; rows beyond the whole mesh are zero. `mesh_receiver`: A mesh row among the device's own 512. `m2g_sender`: A row of the device's extended mesh rows, as for mesh_sender. `m2g_receiver`: A grid row among the device's own 512.
All inputs are finite; a program needn't handle non-finite values.
Results may differ from the reference program's by a relative error of at most 0.0095.
Values may be sent and summed in bfloat16 or wider, within the bound.
A program may use at most 64 MiB of HBM per device.

```python
import jax
import jax.numpy as jnp
from jax import lax

D = 512
H = 512
G_DEV = 512
M_DEV = 512
HALO = 128
CAP = 128
LAYERS = 1
SHARDS = 16
G2M_DEV = 1024
EDGE_DEV = 2048
M2G_DEV = 1536
GRID = 8192
MESH = 8192


def draw_g2m_slot(key, part):
    key = jax.random.fold_in(key, 11)

    def one_device(device_index):
        device_key = jax.random.fold_in(key, device_index)
        first_slots = jnp.arange(3 * CAP, dtype=jnp.int32)
        more_slots = jax.random.randint(jax.random.fold_in(device_key, 1), (G2M_DEV - 3 * CAP,), 0, 3 * CAP, dtype=jnp.int32)
        slot_ids = jax.random.permutation(jax.random.fold_in(device_key, 2), jnp.concatenate([first_slots, more_slots]))
        block_ids = slot_ids // CAP
        lowest = jnp.where(device_index == 0, 1, 0)
        highest = jnp.where(device_index == SHARDS - 1, 1, 2)
        return jnp.clip(block_ids, lowest, highest) * CAP + slot_ids % CAP
    return jax.vmap(one_device)(jnp.arange(SHARDS, dtype=jnp.int32)).reshape(-1)


def with_ends(result, own_key, smallest, largest):
    extent = result.shape
    spot = [jax.random.randint(jax.random.fold_in(own_key, axis), (), 0, extent[axis]) for axis in range(len(extent))]
    result = result.at[tuple(spot)].set(smallest)
    longest = extent.index(max(extent))
    spot[longest] = (spot[longest] + 1) % extent[longest]
    return result.at[tuple(spot)].set(largest)


def levels(stream_key, dims, split, low, high):
    def one(position, blocks):
        heights = jax.random.uniform(jax.random.fold_in(jax.random.fold_in(stream_key, 6), position), (blocks,), jnp.float32, low / len(split), high / len(split))
        return jnp.repeat(jnp.exp(heights), dims[position] // blocks).reshape((-1,) + (1,) * (len(dims) - position - 1))

    loudness = one(*split[0])
    for cut in split[1:]:
        loudness = loudness * one(*cut)
    return loudness


def bell_draw(key, shape, width, limit, pieces=(), kind=jnp.bfloat16):
    result = jax.random.normal(key, shape, jnp.float32) * width
    if len(pieces) > 0:
        result = levels(key, shape, pieces, -0.22, 0.18) * result
    return jnp.clip(result, min=-limit, max=limit).astype(kind)


def setup_inputs(seed: int = 0, part: int = 0) -> dict:
    streams_of = jax.random.split(jax.random.key(seed), 31)
    own_keys = jax.random.split(jax.random.fold_in(streams_of[30], part), 31)
    grid_state = bell_draw(own_keys[0], (GRID, D), 1.0, 6.0, ((0, 16),))
    mesh_state = bell_draw(own_keys[1], (MESH, D), 1.0, 6.0, ((0, 16),))
    g2m_sender = with_ends(jax.random.randint(streams_of[2], (G2M_DEV * SHARDS,), 0, G_DEV), jax.random.fold_in(streams_of[2], 1), 0, G_DEV - 1).astype(jnp.int32)
    g2m_slot = draw_g2m_slot(jax.random.fold_in(streams_of[30], 71), part)
    g2m_land = with_ends(jax.random.randint(streams_of[4], (SHARDS * 3 * CAP,), 0, M_DEV), jax.random.fold_in(streams_of[4], 1), 0, M_DEV - 1).astype(jnp.int32)
    mesh_sender = with_ends(jax.random.randint(streams_of[5], (EDGE_DEV * SHARDS,), 0, M_DEV + 2 * HALO), jax.random.fold_in(streams_of[5], 1), 0, (M_DEV + 2 * HALO) - 1).astype(jnp.int32)
    mesh_receiver = with_ends(jax.random.randint(streams_of[6], (EDGE_DEV * SHARDS,), 0, M_DEV), jax.random.fold_in(streams_of[6], 1), 0, M_DEV - 1).astype(jnp.int32)
    m2g_sender = with_ends(jax.random.randint(streams_of[7], (M2G_DEV * SHARDS,), 0, M_DEV + 2 * HALO), jax.random.fold_in(streams_of[7], 1), 0, (M_DEV + 2 * HALO) - 1).astype(jnp.int32)
    m2g_receiver = with_ends(jax.random.randint(streams_of[8], (M2G_DEV * SHARDS,), 0, G_DEV), jax.random.fold_in(streams_of[8], 1), 0, G_DEV - 1).astype(jnp.int32)
    enc_msg_w1 = bell_draw(streams_of[9], (D, H), D ** -0.5, 0.25, ((0, 4),))
    enc_msg_b1 = bell_draw(streams_of[10], (H,), 0.5, 3.0, (), jnp.float32)
    enc_msg_w2 = bell_draw(streams_of[11], (H, D), H ** -0.5, 0.25, ((0, 4),))
    enc_node_w1 = bell_draw(streams_of[12], (2 * D, H), (2 * D) ** -0.5, 0.1875, ((0, 4),))
    enc_node_b1 = bell_draw(streams_of[13], (H,), 0.5, 3.0, (), jnp.float32)
    enc_node_w2 = bell_draw(streams_of[14], (H, D), H ** -0.5, 0.25, ((0, 4),))
    enc_gain = jnp.clip(1.0 + 0.18 * jax.random.normal(streams_of[15], (D,), jnp.float32), 0.1, 1.9)
    proc_msg_w1 = bell_draw(streams_of[16], (LAYERS, 2 * D, H), (2 * D) ** -0.5, 0.1875, ((1, 4),))
    proc_msg_b1 = bell_draw(streams_of[17], (LAYERS, H), 0.5, 3.0, (), jnp.float32)
    proc_msg_w2 = bell_draw(streams_of[18], (LAYERS, H, D), H ** -0.5, 0.25, ((1, 4),))
    proc_node_w1 = bell_draw(streams_of[19], (LAYERS, 2 * D, H), (2 * D) ** -0.5, 0.1875, ((1, 4),))
    proc_node_b1 = bell_draw(streams_of[20], (LAYERS, H), 0.5, 3.0, (), jnp.float32)
    proc_node_w2 = bell_draw(streams_of[21], (LAYERS, H, D), H ** -0.5, 0.25, ((1, 4),))
    proc_gain = jnp.clip(1.0 + 0.18 * jax.random.normal(streams_of[22], (LAYERS, D), jnp.float32), 0.1, 1.9)
    dec_msg_w1 = bell_draw(streams_of[23], (2 * D, H), (2 * D) ** -0.5, 0.1875, ((0, 4),))
    dec_msg_b1 = bell_draw(streams_of[24], (H,), 0.5, 3.0, (), jnp.float32)
    dec_msg_w2 = bell_draw(streams_of[25], (H, D), H ** -0.5, 0.25, ((0, 4),))
    dec_node_w1 = bell_draw(streams_of[26], (2 * D, H), (2 * D) ** -0.5, 0.1875, ((0, 4),))
    dec_node_b1 = bell_draw(streams_of[27], (H,), 0.5, 3.0, (), jnp.float32)
    dec_node_w2 = bell_draw(streams_of[28], (H, D), H ** -0.5, 0.25, ((0, 4),))
    dec_gain = jnp.clip(1.0 + 0.18 * jax.random.normal(streams_of[29], (D,), jnp.float32), 0.1, 1.9)
    return dict(grid_state=grid_state, mesh_state=mesh_state, g2m_sender=g2m_sender, g2m_slot=g2m_slot, g2m_land=g2m_land, mesh_sender=mesh_sender, mesh_receiver=mesh_receiver, m2g_sender=m2g_sender, m2g_receiver=m2g_receiver, enc_msg_w1=enc_msg_w1, enc_msg_b1=enc_msg_b1, enc_msg_w2=enc_msg_w2, enc_node_w1=enc_node_w1, enc_node_b1=enc_node_b1, enc_node_w2=enc_node_w2, enc_gain=enc_gain, proc_msg_w1=proc_msg_w1, proc_msg_b1=proc_msg_b1, proc_msg_w2=proc_msg_w2, proc_node_w1=proc_node_w1, proc_node_b1=proc_node_b1, proc_node_w2=proc_node_w2, proc_gain=proc_gain, dec_msg_w1=dec_msg_w1, dec_msg_b1=dec_msg_b1, dec_msg_w2=dec_msg_w2, dec_node_w1=dec_node_w1, dec_node_b1=dec_node_b1, dec_node_w2=dec_node_w2, dec_gain=dec_gain)


def layer_norm(values, gain_row):
    average = lax.optimization_barrier(jnp.mean(values, axis=1, keepdims=True))
    centred = values - average
    spread = lax.optimization_barrier(jnp.mean(centred * centred, axis=1, keepdims=True))
    return centred * lax.rsqrt(spread + 1e-05) * gain_row

def node_update(latent, summed, message_out, node_in, node_bias, node_out, gain_row):
    summed_narrow = summed.astype(jnp.bfloat16)
    incoming = jnp.dot(summed_narrow, message_out, preferred_element_type=jnp.float32)
    incoming_narrow = incoming.astype(jnp.bfloat16)
    before = jnp.dot(latent, node_in[:D], preferred_element_type=jnp.float32)
    before = before + jnp.dot(incoming_narrow, node_in[D:], preferred_element_type=jnp.float32) + node_bias
    hidden = jax.nn.silu(before).astype(jnp.bfloat16)
    mixed_out = jnp.dot(hidden, node_out, preferred_element_type=jnp.float32)
    return (latent.astype(jnp.float32) + layer_norm(mixed_out, gain_row)).astype(jnp.bfloat16)

def device_rows(local, per_device, count):
    offsets = jnp.arange(SHARDS, dtype=jnp.int32) * per_device
    return (local.reshape(SHARDS, count) + offsets[:, None]).reshape(-1).astype(jnp.int32)

def edge_sum(framed_terms, target_terms, senders, receivers, unit_bias, row_count):
    before = framed_terms[senders] + target_terms[receivers] + unit_bias
    return jax.ops.segment_sum(jax.nn.silu(before), receivers, num_segments=row_count)

def reference(grid_state, mesh_state, g2m_sender, g2m_slot, g2m_land, mesh_sender, mesh_receiver, m2g_sender, m2g_receiver, enc_msg_w1, enc_msg_b1, enc_msg_w2, enc_node_w1, enc_node_b1, enc_node_w2, enc_gain, proc_msg_w1, proc_msg_b1, proc_msg_w2, proc_node_w1, proc_node_b1, proc_node_w2, proc_gain, dec_msg_w1, dec_msg_b1, dec_msg_w2, dec_node_w1, dec_node_b1, dec_node_w2, dec_gain):
    grid_hidden = jax.nn.silu(jnp.dot(grid_state, enc_msg_w1, preferred_element_type=jnp.float32) + enc_msg_b1)
    source_rows = device_rows(g2m_sender, G_DEV, G2M_DEV)
    slot_ids = device_rows(g2m_slot, 3 * CAP, G2M_DEV)
    blocks = jax.ops.segment_sum(grid_hidden[source_rows], slot_ids, num_segments=SHARDS * 3 * CAP)
    blocks = blocks.reshape(SHARDS, 3, CAP, H)
    empty_block = jnp.zeros((1, 3, CAP, H), jnp.float32)
    framed_blocks = jnp.concatenate([empty_block, blocks, empty_block], axis=0)
    incoming = jnp.stack([framed_blocks[2:SHARDS + 2, 0], framed_blocks[1:SHARDS + 1, 1], framed_blocks[0:SHARDS, 2]], axis=1)
    targets = device_rows(g2m_land, M_DEV, 3 * CAP)
    enc_hidden = jax.ops.segment_sum(incoming.reshape(SHARDS * 3 * CAP, H), targets, num_segments=MESH)
    mesh_latent = node_update(mesh_state, enc_hidden, enc_msg_w2, enc_node_w1, enc_node_b1, enc_node_w2, enc_gain)
    senders = device_rows(mesh_sender, M_DEV, EDGE_DEV)
    receivers = device_rows(mesh_receiver, M_DEV, EDGE_DEV)
    for layer in range(LAYERS):
        framed = jnp.pad(mesh_latent, ((HALO, HALO), (0, 0)))
        weights_in = proc_msg_w1[layer]
        framed_terms = jnp.dot(framed, weights_in[:D], preferred_element_type=jnp.float32)
        local_terms = jnp.dot(mesh_latent, weights_in[D:], preferred_element_type=jnp.float32)
        proc_hidden = edge_sum(framed_terms, local_terms, senders, receivers, proc_msg_b1[layer], MESH)
        mesh_latent = node_update(mesh_latent, proc_hidden, proc_msg_w2[layer], proc_node_w1[layer], proc_node_b1[layer], proc_node_w2[layer], proc_gain[layer])
    framed = jnp.pad(mesh_latent, ((HALO, HALO), (0, 0)))
    framed_terms = jnp.dot(framed, dec_msg_w1[:D], preferred_element_type=jnp.float32)
    grid_terms = jnp.dot(grid_state, dec_msg_w1[D:], preferred_element_type=jnp.float32)
    grid_senders = device_rows(m2g_sender, M_DEV, M2G_DEV)
    grid_receivers = device_rows(m2g_receiver, G_DEV, M2G_DEV)
    dec_hidden = edge_sum(framed_terms, grid_terms, grid_senders, grid_receivers, dec_msg_b1, GRID)
    return node_update(grid_state, dec_hidden, dec_msg_w2, dec_node_w1, dec_node_b1, dec_node_w2, dec_gain)
```

```python
import functools

import jax
import jax.numpy as jnp
from jax import lax
from jax.experimental import pallas as pl
from jax.experimental.pallas import tpu as pltpu
from jax.sharding import PartitionSpec as P

HALO = 128
LANES = 128
F32 = jnp.float32
BF16 = jnp.bfloat16
MESH = pl.DeviceIdType.MESH

GROUPS = ((0,), (1, 2, 3), (4, 5, 6, 7), (8, 9, 10, 11))


def silu(v):
    h = 0.5 * v
    return h + h * jnp.tanh(h)


def dot(a, b):
    return jnp.dot(a, b, preferred_element_type=F32)


def kernel(dims, plan, *refs):
    bands, feats, subs = dims
    (
        grid_hbm, mesh_hbm, g2m_s, g2m_q, g2m_l, mesh_s, mesh_r, m2g_s, m2g_r,
        enc_b1, enc_nb, enc_gain, proc_b1, proc_nb, proc_gain, dec_b1, dec_nb, dec_gain,
    ) = refs[:18]
    shards = refs[18:30]
    out_ref = refs[30]
    (
        w0, w1, w2, w3, grid, mesh, inc, slots_out, framed_a, framed_b, counts,
        oh_g, oht_q, land, oh_m, oht_m, oh_d, oht_d, terms, terms_d, msg,
        zsend, zrecv, psend, precv, dsend, drecv, wsem, ssem, hsend, hrecv,
    ) = refs[31:]
    wbufs = (w0, w1, w2, w3)
    y = lax.axis_index("ens")
    z = lax.axis_index("band")
    x = lax.axis_index("feat")
    c = lax.axis_index("sub")
    xn = x + 1 - 2 * lax.rem(x, 2)
    yn = 1 - y
    q = 2 * y + lax.rem(x, 2)
    position = (z * feats + x) * subs + c
    last = bands * feats * subs - 1
    has_left = position > 0
    has_right = position < last

    def place(number):
        return (y, number // (feats * subs), lax.rem(number // subs, feats), lax.rem(number, subs))

    left = place(lax.rem(position + last, last + 1))
    right = place(lax.rem(position + 1, last + 1))
    sibling = (y, z, x, 1 - c)
    peers = ((y, z, xn, c), (yn, z, x, c), (yn, z, xn, c))
    chunks = (2 * y + lax.rem(xn, 2), 2 * yn + lax.rem(x, 2), 2 * yn + lax.rem(xn, 2))

    local = []
    for g, members in enumerate(GROUPS):
        group = []
        for m in members:
            off, rows = plan[m]
            group.append(
                pltpu.make_async_copy(
                    shards[m], wbufs[g].at[z, pl.ds(off, rows), :], wsem.at[m]
                )
            )
        local.append(group)
    states = (
        pltpu.make_async_copy(grid_hbm, grid, ssem.at[0]),
        pltpu.make_async_copy(mesh_hbm, mesh, ssem.at[1]),
    )
    for group in local:
        for copy in group:
            copy.start()
    for copy in states:
        copy.start()

    barrier = pltpu.get_barrier_semaphore()

    def greet(r, carry):
        pl.semaphore_signal(
            barrier, inc=1, device_id=(y, lax.rem(z + r, bands), x, c), device_id_type=MESH
        )
        return carry

    lax.fori_loop(1, bands, greet, 0)
    for peer in peers:
        pl.semaphore_signal(barrier, inc=1, device_id=peer, device_id_type=MESH)
    for peer in (sibling, left, right):
        pl.semaphore_signal(barrier, inc=1, device_id=peer, device_id_type=MESH)
    pl.semaphore_wait(barrier, bands - 1 + 6)

    def half_rows(g, core):
        half = wbufs[g].shape[1] // 2
        return pl.ds(pl.multiple_of(core * half, 16), half)

    def cols(chunk):
        width = wbufs[0].shape[2] // 4
        return pl.ds(pl.multiple_of(chunk * width, LANES), width)

    def z_copy(g, r, owner, target):
        piece = wbufs[g].at[owner, half_rows(g, c), cols(q)]
        return pltpu.make_async_remote_copy(
            piece, piece, zsend.at[g, r], zrecv.at[g, r],
            device_id=(y, target, x, c), device_id_type=MESH,
        )

    def p_copy(g, r, owner, j, chunk):
        piece = wbufs[g].at[owner, half_rows(g, c), cols(chunk)]
        return pltpu.make_async_remote_copy(
            piece, piece, psend.at[g, r, j], precv.at[g, r, j],
            device_id=peers[j], device_id_type=MESH,
        )

    def d_copy(g, r, owner, core):
        piece = wbufs[g].at[owner, half_rows(g, core), :]
        return pltpu.make_async_remote_copy(
            piece, piece, dsend.at[g, r], drecv.at[g, r],
            device_id=sibling, device_id_type=MESH,
        )

    def each(body):
        def step(r, carry):
            body(r, lax.rem(z - r + bands, bands))
            return carry

        lax.fori_loop(1, bands, step, 0)

    def z_start(g):
        for copy in local[g]:
            copy.wait()
        each(lambda r, owner: z_copy(g, r, z, lax.rem(z + r, bands)).start())

    def z_pass(g):
        def body(r, owner):
            z_copy(g, r, owner, owner).wait_recv()
            for j in range(3):
                p_copy(g, r, owner, j, q).start()

        each(body)

    def p_pass(g):
        def body(r, owner):
            for j in range(3):
                p_copy(g, r, owner, j, chunks[j]).wait_recv()
            d_copy(g, r, owner, c).start()

        each(body)

    def d_wait(g):
        each(lambda r, owner: d_copy(g, r, owner, 1 - c).wait_recv())

    def finish(g):
        def body(r, owner):
            z_copy(g, r, z, lax.rem(z + r, bands)).wait_send()
            for j in range(3):
                p_copy(g, r, owner, j, q).wait_send()
            d_copy(g, r, owner, c).wait_send()

        each(body)

    def weight(g, m, first=0, count=None):
        off, rows = plan[m]
        whole = wbufs[g][:, off : off + rows, :]
        return whole.reshape(bands * rows, whole.shape[2])

    def exchange(step, to_left, from_right, to_right, from_left):
        def left_copy():
            return pltpu.make_async_remote_copy(
                to_left, from_right, hsend.at[step, 0], hrecv.at[step, 0],
                device_id=left, device_id_type=MESH,
            )

        def right_copy():
            return pltpu.make_async_remote_copy(
                to_right, from_left, hsend.at[step, 1], hrecv.at[step, 1],
                device_id=right, device_id_type=MESH,
            )

        def start():
            @pl.when(has_left)
            def _():
                left_copy().start()

            @pl.when(has_right)
            def _():
                right_copy().start()

        def wait():
            @pl.when(has_right)
            def _():
                left_copy().wait_recv()

            @pl.when(has_left)
            def _():
                right_copy().wait_recv()

        def done():
            @pl.when(has_left)
            def _():
                left_copy().wait_send()

            @pl.when(has_right)
            def _():
                right_copy().wait_send()

        return start, wait, done

    cap = inc.shape[0] // 3
    rows_m = mesh.shape[0]
    width = mesh.shape[1]
    slot_x = exchange(
        0, slots_out.at[pl.ds(0, cap)], inc.at[pl.ds(0, cap)],
        slots_out.at[pl.ds(cap, cap)], inc.at[pl.ds(2 * cap, cap)],
    )
    rims = tuple(
        exchange(
            1 + i, buf.at[pl.ds(HALO, HALO)], buf.at[pl.ds(HALO + rows_m, HALO)],
            buf.at[pl.ds(rows_m, HALO)], buf.at[pl.ds(0, HALO)],
        )
        for i, buf in enumerate((framed_a, framed_b))
    )

    @pl.when(jnp.logical_not(has_left))
    def _():
        inc[2 * cap : 3 * cap] = jnp.zeros((cap, width), BF16)
        framed_a[0:HALO] = jnp.zeros((HALO, width), BF16)
        framed_b[0:HALO] = jnp.zeros((HALO, width), BF16)

    @pl.when(jnp.logical_not(has_right))
    def _():
        inc[0:cap] = jnp.zeros((cap, width), BF16)
        framed_a[HALO + rows_m :] = jnp.zeros((HALO, width), BF16)
        framed_b[HALO + rows_m :] = jnp.zeros((HALO, width), BF16)

    def pick_rows(target, base, row, first, count):
        column = jnp.broadcast_to(row.astype(F32), (LANES, LANES)).T
        for j in range(count // LANES):
            lane = lax.broadcasted_iota(jnp.int32, (LANES, LANES), 1) + j * LANES
            target[pl.ds(base, LANES), first + j * LANES : first + (j + 1) * LANES] = jnp.where(
                column == lane.astype(F32), 1.0, 0.0
            ).astype(BF16)

    def pick_cols(target, base, row, count):
        sub = lax.broadcasted_iota(jnp.int32, (count, LANES), 0)
        target[:, pl.ds(base, LANES)] = jnp.where(
            sub == jnp.broadcast_to(row, (count, LANES)), 1.0, 0.0
        ).astype(BF16)

    def blocks(count, body):
        def step(e, carry):
            body(e, pl.multiple_of(e * LANES, LANES))
            return carry

        lax.fori_loop(0, count, step, 0)

    def g2m_block(e, base):
        pick_rows(oh_g, base, g2m_s[pl.ds(e, 1), :], 0, oh_g.shape[1])
        pick_cols(oht_q, base, g2m_q[pl.ds(e, 1), :], oht_q.shape[0])

    def mesh_block(e, base):
        row = mesh_r[pl.ds(e, 1), :]
        pick_rows(oh_m, base, mesh_s[pl.ds(e, 1), :], 0, framed_a.shape[0])
        pick_rows(oh_m, base, row, framed_a.shape[0], rows_m)
        pick_cols(oht_m, base, row, rows_m)

    def m2g_block(e, base):
        row = m2g_r[pl.ds(e, 1), :]
        pick_rows(oh_d, base, m2g_s[pl.ds(e, 1), :], 0, framed_a.shape[0])
        pick_rows(oh_d, base, row, framed_a.shape[0], grid.shape[0])
        pick_cols(oht_d, base, row, grid.shape[0])

    def update(v, a, g, names, bias, gain_row):
        message_out, node_in, node_out = (weight(g, m) for m in names)
        incoming = dot(a.astype(BF16), message_out).astype(BF16)
        before = dot(v, node_in[:width]) + dot(incoming, node_in[width:]) + bias[...]
        mixed = dot(silu(before).astype(BF16), node_out)
        centred = mixed - jnp.mean(mixed, axis=1, keepdims=True)
        spread = jnp.mean(centred * centred, axis=1, keepdims=True)
        return (v.astype(F32) + centred * lax.rsqrt(spread + 1e-05) * gain_row[...]).astype(BF16)

    def outer(ref, base=0):
        return jnp.concatenate(
            [ref[base : base + HALO], ref[base + rows_m - HALO : base + rows_m]], axis=0
        )

    def inner(ref, base=0):
        return ref[base + HALO : base + rows_m - HALO]

    def messages(oh, table, count):
        size = 256

        def step(e, carry):
            base = pl.multiple_of(e * size, size)
            msg[pl.ds(base, size), :] = silu(dot(oh[pl.ds(base, size), :], table[...])).astype(BF16)
            return carry

        lax.fori_loop(0, count // size, step, 0)

    z_start(0)
    z_start(1)
    blocks(g2m_s.shape[0], g2m_block)
    z_pass(0)
    counts[...] = dot(oht_q[...], oh_g[...]).astype(BF16)
    for k in range(3):
        pick_cols(land, k * LANES, g2m_l[:, k * LANES : (k + 1) * LANES], rows_m)
    p_pass(0)
    z_pass(1)
    z_start(2)
    blocks(mesh_s.shape[0], mesh_block)
    d_wait(0)
    p_pass(1)
    for copy in states:
        copy.wait()
    hidden = silu(dot(grid[...], weight(0, 0)) + enc_b1[...]).astype(BF16)
    slot_sum = dot(counts[...], hidden).astype(BF16)
    slots_out[0:cap] = slot_sum[0:cap]
    slots_out[cap : 2 * cap] = slot_sum[2 * cap : 3 * cap]
    slot_x[0]()
    inc[cap : 2 * cap] = slot_sum[cap : 2 * cap]
    z_pass(2)
    z_start(3)
    d_wait(1)
    slot_x[1]()
    names = (1, 2, 3)
    arrived = dot(outer(land), inc[...])
    new = update(outer(mesh), arrived, 1, names, enc_nb, enc_gain)
    framed_a[HALO : 2 * HALO] = new[:HALO]
    framed_a[rows_m : HALO + rows_m] = new[HALO:]
    rims[0][0]()
    arrived = dot(inner(land), inc[...])
    framed_a[2 * HALO : rows_m] = update(inner(mesh), arrived, 1, names, enc_nb, enc_gain)
    p_pass(2)
    blocks(m2g_s.shape[0], m2g_block)
    z_pass(3)
    d_wait(2)
    w_in = weight(2, 4)
    own = framed_a[HALO : HALO + rows_m]
    ext = framed_a.shape[0]
    terms[HALO : HALO + rows_m] = dot(own, w_in[:width]).astype(BF16)
    terms[ext:] = (dot(own, w_in[width:]) + proc_b1[...]).astype(BF16)
    rims[0][1]()
    rim = jnp.concatenate([framed_a[0:HALO], framed_a[HALO + rows_m :]], axis=0)
    rim_terms = dot(rim, w_in[:width]).astype(BF16)
    terms[0:HALO] = rim_terms[:HALO]
    terms[HALO + rows_m : ext] = rim_terms[HALO:]
    messages(oh_m, terms, oh_m.shape[0])
    p_pass(3)
    names = (5, 6, 7)
    count = oh_m.shape[0]
    arrived = dot(outer(oht_m), msg[0:count])
    new = update(outer(framed_a, HALO), arrived, 2, names, proc_nb, proc_gain)
    framed_b[HALO : 2 * HALO] = new[:HALO]
    framed_b[rows_m : HALO + rows_m] = new[HALO:]
    rims[1][0]()
    arrived = dot(inner(oht_m), msg[0:count])
    framed_b[2 * HALO : rows_m] = update(
        inner(framed_a, HALO), arrived, 2, names, proc_nb, proc_gain
    )
    d_wait(3)
    w_in = weight(3, 8)
    terms_d[ext:] = (dot(grid[...], w_in[width:]) + dec_b1[...]).astype(BF16)
    terms_d[HALO : HALO + rows_m] = dot(framed_b[HALO : HALO + rows_m], w_in[:width]).astype(BF16)
    rims[1][1]()
    rim = jnp.concatenate([framed_b[0:HALO], framed_b[HALO + rows_m :]], axis=0)
    rim_terms = dot(rim, w_in[:width]).astype(BF16)
    terms_d[0:HALO] = rim_terms[:HALO]
    terms_d[HALO + rows_m : ext] = rim_terms[HALO:]
    messages(oh_d, terms_d, oh_d.shape[0])
    names = (9, 10, 11)
    count = oh_d.shape[0]
    middle = grid.shape[0] // 2
    for lo in (0, middle):
        part = slice(lo, lo + middle)
        arrived = dot(oht_d[part], msg[0:count])
        out_ref[part] = update(grid[part], arrived, 3, names, dec_nb, dec_gain)
    for g in range(4):
        finish(g)
    for moves in (slot_x, *rims):
        moves[2]()


def on_device(
    dims,
    grid_state, mesh_state, g2m_sender, g2m_slot, g2m_land,
    mesh_sender, mesh_receiver, m2g_sender, m2g_receiver,
    enc_msg_w1, enc_msg_b1, enc_msg_w2, enc_node_w1, enc_node_b1, enc_node_w2, enc_gain,
    proc_msg_w1, proc_msg_b1, proc_msg_w2, proc_node_w1, proc_node_b1, proc_node_w2, proc_gain,
    dec_msg_w1, dec_msg_b1, dec_msg_w2, dec_node_w1, dec_node_b1, dec_node_w2, dec_gain,
):
    bands = dims[0]
    weights = (
        enc_msg_w1, enc_msg_w2, enc_node_w1, enc_node_w2,
        proc_msg_w1[0], proc_msg_w2[0], proc_node_w1[0], proc_node_w2[0],
        dec_msg_w1, dec_msg_w2, dec_node_w1, dec_node_w2,
    )
    width = grid_state.shape[1]
    rows_g, rows_m = grid_state.shape[0], mesh_state.shape[0]
    slots = g2m_land.shape[0]
    ext = rows_m + 2 * HALO
    plan = {}
    buffers = []
    for members in GROUPS:
        off = 0
        for m in members:
            rows = weights[m].shape[0]
            plan[m] = (off, rows)
            off += rows
        buffers.append(pltpu.VMEM((bands, -(-off // 32) * 32, width), BF16))
    groups = len(GROUPS)
    e_g, e_m, e_d = g2m_sender.shape[0], mesh_sender.shape[0], m2g_sender.shape[0]
    dma = pltpu.SemaphoreType.DMA
    scratch = buffers + [
        pltpu.VMEM((rows_g, width), BF16),
        pltpu.VMEM((rows_m, width), BF16),
        pltpu.VMEM((slots, width), BF16),
        pltpu.VMEM((2 * slots // 3, width), BF16),
        pltpu.VMEM((ext, width), BF16),
        pltpu.VMEM((ext, width), BF16),
        pltpu.VMEM((slots, rows_g), BF16),
        pltpu.VMEM((e_g, rows_g), BF16),
        pltpu.VMEM((slots, e_g), BF16),
        pltpu.VMEM((rows_m, slots), BF16),
        pltpu.VMEM((e_m, ext + rows_m), BF16),
        pltpu.VMEM((rows_m, e_m), BF16),
        pltpu.VMEM((e_d, ext + rows_g), BF16),
        pltpu.VMEM((rows_g, e_d), BF16),
        pltpu.VMEM((ext + rows_m, width), BF16),
        pltpu.VMEM((ext + rows_g, width), BF16),
        pltpu.VMEM((max(e_m, e_d), width), BF16),
        dma((groups, bands)),
        dma((groups, bands)),
        dma((groups, bands, 3)),
        dma((groups, bands, 3)),
        dma((groups, bands)),
        dma((groups, bands)),
        dma((12,)),
        dma((2,)),
        dma((3, 2)),
        dma((3, 2)),
    ]
    table = lambda v: v.reshape(-1, LANES)
    row = lambda v: v.reshape(1, -1)
    hbm = pl.BlockSpec(memory_space=pl.ANY)
    vmem = pl.BlockSpec(memory_space=pltpu.VMEM)
    return pl.pallas_call(
        functools.partial(kernel, dims, plan),
        out_shape=jax.ShapeDtypeStruct((rows_g, width), BF16),
        in_specs=[hbm] * 2 + [vmem] * 16 + [hbm] * 12,
        out_specs=vmem,
        scratch_shapes=scratch,
        compiler_params=pltpu.CompilerParams(
            collective_id=0, has_side_effects=True, vmem_limit_bytes=52 * 1024 * 1024
        ),
    )(
        grid_state, mesh_state, table(g2m_sender), table(g2m_slot), row(g2m_land),
        table(mesh_sender), table(mesh_receiver), table(m2g_sender), table(m2g_receiver),
        row(enc_msg_b1), row(enc_node_b1), row(enc_gain),
        proc_msg_b1, proc_node_b1, proc_gain,
        row(dec_msg_b1), row(dec_node_b1), row(dec_gain),
        *weights,
    )


def solution(mesh):
    rows = P(("ens", "band", "feat", "sub"), None)
    edges = P(("band", "feat", "sub"))
    flat = P("band", None)
    deep = P(None, "band", None)
    enc = (flat, P(), flat, flat, P(), flat, P())
    proc = (deep, P(), deep, deep, P(), deep, P())
    in_specs = (rows, rows) + (edges,) * 7 + enc + proc + enc
    dims = (mesh.shape["band"], mesh.shape["feat"], mesh.shape["sub"])
    return jax.shard_map(
        functools.partial(on_device, dims),
        mesh=mesh, in_specs=in_specs, out_specs=rows, check_vma=False,
    )
```

```python
import functools

import jax
import jax.numpy as jnp
from jax import lax
from jax.experimental import pallas as pl
from jax.experimental.pallas import tpu as pltpu
from jax.sharding import PartitionSpec as P

HALO = 128
LANES = 128
VMEM_LIMIT = 60 * 1024 * 1024
F32 = jnp.float32
BF16 = jnp.bfloat16
MESH = pl.DeviceIdType.MESH

GROUPS = ((0,), (1, 2, 3), (4, 5, 6, 7), (8, 9, 10, 11))


DIRECT = (0,)


def silu(v):
    h = 0.5 * v
    return h + h * jnp.tanh(h)


def dot(a, b):
    return jnp.dot(a, b, preferred_element_type=F32)


def kernel(dims, plan, *refs):
    bands, feats, subs = dims
    grid_hbm, mesh_hbm = refs[:2]
    small_hbm = refs[2:18]
    shards = refs[18:30]
    out_ref = refs[30]
    (
        w0, w1, w2, w3, grid, mesh, inc, slots_out, framed_a, framed_b, counts,
        oh_g, oht_q, land, oh_m, oht_m, oh_d, oht_d, terms, terms_d, msg,
        zsend, zrecv, psend, precv, fsend, frecv, dsend, drecv,
        wsem, ssem, nsem, hsend, hrecv,
    ) = refs[31:-16]
    (
        g2m_s, g2m_q, g2m_l, mesh_s, mesh_r, m2g_s, m2g_r,
        enc_b1, enc_nb, enc_gain, proc_b1, proc_nb, proc_gain, dec_b1, dec_nb, dec_gain,
    ) = refs[-16:]
    wbufs = (w0, w1, w2, w3)
    y = lax.axis_index("ens")
    z = lax.axis_index("band")
    x = lax.axis_index("feat")
    c = lax.axis_index("sub")
    xn = x + 1 - 2 * lax.rem(x, 2)
    yn = 1 - y
    q = 2 * y + lax.rem(x, 2)
    position = (z * feats + x) * subs + c
    last = bands * feats * subs - 1
    has_left = position > 0
    has_right = position < last

    def place(number):
        return (y, number // (feats * subs), lax.rem(number // subs, feats), lax.rem(number, subs))

    left = place(lax.rem(position + last, last + 1))
    right = place(lax.rem(position + 1, last + 1))
    sibling = (y, z, x, 1 - c)
    peers = ((y, z, xn, c), (yn, z, x, c), (yn, z, xn, c))
    chunks = (2 * y + lax.rem(xn, 2), 2 * yn + lax.rem(x, 2), 2 * yn + lax.rem(xn, 2))

    local = []
    for g, members in enumerate(GROUPS):
        group = []
        for m in members:
            off, rows = plan[m]
            group.append(
                pltpu.make_async_copy(
                    shards[m], wbufs[g].at[z, pl.ds(off, rows), :], wsem.at[m]
                )
            )
        local.append(group)
    states = (
        pltpu.make_async_copy(grid_hbm, grid, ssem.at[0]),
        pltpu.make_async_copy(mesh_hbm, mesh, ssem.at[1]),
    )
    for group in local:
        for copy in group:
            copy.start()
    small = [
        pltpu.make_async_copy(src, dst, nsem.at[i])
        for i, (src, dst) in enumerate(zip(small_hbm, refs[-16:]))
    ]
    for copy in small:
        copy.start()
    for copy in states:
        copy.start()

    barrier = pltpu.get_barrier_semaphore()

    def greet(r, carry):
        pl.semaphore_signal(
            barrier, inc=1, device_id=(y, lax.rem(z + r, bands), x, c), device_id_type=MESH
        )
        return carry

    lax.fori_loop(1, bands, greet, 0)
    for peer in peers:
        pl.semaphore_signal(barrier, inc=1, device_id=peer, device_id_type=MESH)
    for peer in (sibling, left, right):
        pl.semaphore_signal(barrier, inc=1, device_id=peer, device_id_type=MESH)
    pl.semaphore_wait(barrier, bands - 1 + 6)

    def half_rows(g, core):
        half = wbufs[g].shape[1] // 2
        return pl.ds(pl.multiple_of(core * half, 16), half)

    def cols(chunk):
        width = wbufs[0].shape[2] // 4
        return pl.ds(pl.multiple_of(chunk * width, LANES), width)

    def z_copy(g, r, owner, target):
        piece = wbufs[g].at[owner, half_rows(g, c), cols(q)]
        return pltpu.make_async_remote_copy(
            piece, piece, zsend.at[g, r], zrecv.at[g, r],
            device_id=(y, target, x, c), device_id_type=MESH,
        )

    def p_copy(g, r, owner, j, chunk):
        piece = wbufs[g].at[owner, half_rows(g, c), cols(chunk)]
        return pltpu.make_async_remote_copy(
            piece, piece, psend.at[g, r, j], precv.at[g, r, j],
            device_id=peers[j], device_id_type=MESH,
        )

    def d_copy(g, r, owner, core):
        piece = wbufs[g].at[owner, half_rows(g, core), :]
        return pltpu.make_async_remote_copy(
            piece, piece, dsend.at[g, r], drecv.at[g, r],
            device_id=sibling, device_id_type=MESH,
        )

    def each(body):
        def step(r, carry):
            body(r, lax.rem(z - r + bands, bands))
            return carry

        lax.fori_loop(1, bands, step, 0)

    def z_start(g):
        for copy in local[g]:
            copy.wait()
        each(lambda r, owner: z_copy(g, r, z, lax.rem(z + r, bands)).start())

    def direct(g):
        return g in DIRECT

    def f_copy(g, r, owner, i, chunk):
        quarter = wbufs[g].shape[1] // 4
        start = pl.multiple_of((2 * c + i) * quarter, 16)
        piece = wbufs[g].at[owner, pl.ds(start, quarter), cols(chunk)]
        return pltpu.make_async_remote_copy(
            piece, piece, fsend.at[g, r, i], frecv.at[g, r, i],
            device_id=peers[1 - i], device_id_type=MESH,
        )

    def z_pass(g):
        def body(r, owner):
            z_copy(g, r, owner, owner).wait_recv()
            for j in range(3 if direct(g) else 2):
                p_copy(g, r, owner, j, q).start()

        each(body)

    def f_pass(g):
        def body(r, owner):
            for i in range(2):
                p_copy(g, r, owner, i, chunks[i]).wait_recv()
                f_copy(g, r, owner, i, chunks[i]).start()

        each(body)

    def p_pass(g):
        def body(r, owner):
            if direct(g):
                for j in range(3):
                    p_copy(g, r, owner, j, chunks[j]).wait_recv()
            else:
                for i in range(2):
                    f_copy(g, r, owner, i, chunks[2]).wait_recv()
            d_copy(g, r, owner, c).start()

        each(body)

    def d_wait(g):
        each(lambda r, owner: d_copy(g, r, owner, 1 - c).wait_recv())

    def finish(g):
        def body(r, owner):
            z_copy(g, r, z, lax.rem(z + r, bands)).wait_send()
            for j in range(3 if direct(g) else 2):
                p_copy(g, r, owner, j, q).wait_send()
            if not direct(g):
                for i in range(2):
                    f_copy(g, r, owner, i, chunks[i]).wait_send()
            d_copy(g, r, owner, c).wait_send()

        each(body)

    def weight(g, m, first=0, count=None):
        off, rows = plan[m]
        whole = wbufs[g][:, off : off + rows, :]
        return whole.reshape(bands * rows, whole.shape[2])

    def exchange(step, to_left, from_right, to_right, from_left):
        def left_copy():
            return pltpu.make_async_remote_copy(
                to_left, from_right, hsend.at[step, 0], hrecv.at[step, 0],
                device_id=left, device_id_type=MESH,
            )

        def right_copy():
            return pltpu.make_async_remote_copy(
                to_right, from_left, hsend.at[step, 1], hrecv.at[step, 1],
                device_id=right, device_id_type=MESH,
            )

        def start():
            @pl.when(has_left)
            def _():
                left_copy().start()

            @pl.when(has_right)
            def _():
                right_copy().start()

        def wait():
            @pl.when(has_right)
            def _():
                left_copy().wait_recv()

            @pl.when(has_left)
            def _():
                right_copy().wait_recv()

        def done():
            @pl.when(has_left)
            def _():
                left_copy().wait_send()

            @pl.when(has_right)
            def _():
                right_copy().wait_send()

        return start, wait, done

    cap = inc.shape[0] // 3
    rows_m = mesh.shape[0]
    width = mesh.shape[1]
    slot_x = exchange(
        0, slots_out.at[pl.ds(0, cap)], inc.at[pl.ds(0, cap)],
        slots_out.at[pl.ds(cap, cap)], inc.at[pl.ds(2 * cap, cap)],
    )
    rims = tuple(
        exchange(
            1 + i, buf.at[pl.ds(HALO, HALO)], buf.at[pl.ds(HALO + rows_m, HALO)],
            buf.at[pl.ds(rows_m, HALO)], buf.at[pl.ds(0, HALO)],
        )
        for i, buf in enumerate((framed_a, framed_b))
    )

    @pl.when(jnp.logical_not(has_left))
    def _():
        inc[2 * cap : 3 * cap] = jnp.zeros((cap, width), BF16)
        framed_a[0:HALO] = jnp.zeros((HALO, width), BF16)
        framed_b[0:HALO] = jnp.zeros((HALO, width), BF16)

    @pl.when(jnp.logical_not(has_right))
    def _():
        inc[0:cap] = jnp.zeros((cap, width), BF16)
        framed_a[HALO + rows_m :] = jnp.zeros((HALO, width), BF16)
        framed_b[HALO + rows_m :] = jnp.zeros((HALO, width), BF16)

    def pick_rows(target, base, row, first, count):
        column = jnp.broadcast_to(row.astype(F32), (LANES, LANES)).T
        for j in range(count // LANES):
            lane = lax.broadcasted_iota(jnp.int32, (LANES, LANES), 1) + j * LANES
            target[pl.ds(base, LANES), first + j * LANES : first + (j + 1) * LANES] = jnp.where(
                column == lane.astype(F32), 1.0, 0.0
            ).astype(BF16)

    def pick_cols(target, base, row, count):
        sub = lax.broadcasted_iota(jnp.int32, (count, LANES), 0)
        target[:, pl.ds(base, LANES)] = jnp.where(
            sub == jnp.broadcast_to(row, (count, LANES)), 1.0, 0.0
        ).astype(BF16)

    def blocks(first, count, body):
        def step(e, carry):
            body(e, pl.multiple_of(e * LANES, LANES))
            return carry

        lax.fori_loop(first, count, step, 0)

    def g2m_block(e, base):
        pick_rows(oh_g, base, g2m_s[pl.ds(e, 1), :], 0, oh_g.shape[1])
        pick_cols(oht_q, base, g2m_q[pl.ds(e, 1), :], oht_q.shape[0])

    def mesh_block(e, base):
        row = mesh_r[pl.ds(e, 1), :]
        pick_rows(oh_m, base, mesh_s[pl.ds(e, 1), :], 0, framed_a.shape[0])
        pick_rows(oh_m, base, row, framed_a.shape[0], rows_m)
        pick_cols(oht_m, base, row, rows_m)

    def m2g_block(e, base):
        row = m2g_r[pl.ds(e, 1), :]
        pick_rows(oh_d, base, m2g_s[pl.ds(e, 1), :], 0, framed_a.shape[0])
        pick_rows(oh_d, base, row, framed_a.shape[0], grid.shape[0])
        pick_cols(oht_d, base, row, grid.shape[0])

    def update(v, a, g, names, bias, gain_row):
        message_out, node_in, node_out = (weight(g, m) for m in names)
        incoming = dot(a.astype(BF16), message_out).astype(BF16)
        before = dot(v, node_in[:width]) + dot(incoming, node_in[width:]) + bias[...]
        mixed = dot(silu(before).astype(BF16), node_out)
        centred = mixed - jnp.mean(mixed, axis=1, keepdims=True)
        spread = jnp.mean(centred * centred, axis=1, keepdims=True)
        return (v.astype(F32) + centred * lax.rsqrt(spread + 1e-05) * gain_row[...]).astype(BF16)

    def outer(ref, base=0):
        return jnp.concatenate(
            [ref[base : base + HALO], ref[base + rows_m - HALO : base + rows_m]], axis=0
        )

    def inner(ref, base=0):
        return ref[base + HALO : base + rows_m - HALO]

    def messages(oh, table, count):
        size = 256

        def step(e, carry):
            base = pl.multiple_of(e * size, size)
            msg[pl.ds(base, size), :] = silu(dot(oh[pl.ds(base, size), :], table[...])).astype(BF16)
            return carry

        lax.fori_loop(0, count // size, step, 0)

    z_start(0)
    z_start(1)
    for copy in small:
        copy.wait()
    blocks(0, g2m_s.shape[0], g2m_block)
    z_pass(0)
    z_start(2)
    counts[...] = dot(oht_q[...], oh_g[...]).astype(BF16)
    for k in range(3):
        pick_cols(land, k * LANES, g2m_l[k * LANES : (k + 1) * LANES].reshape(1, LANES), rows_m)
    p_pass(0)
    z_pass(1)
    n_m, n_d = mesh_s.shape[0], m2g_s.shape[0]
    blocks(0, n_m // 4, mesh_block)
    for copy in states:
        copy.wait()
    d_wait(0)
    hidden = silu(dot(grid[...], weight(0, 0)) + enc_b1[...]).astype(BF16)
    slot_sum = dot(counts[...], hidden).astype(BF16)
    slots_out[0:cap] = slot_sum[0:cap]
    slots_out[cap : 2 * cap] = slot_sum[2 * cap : 3 * cap]
    slot_x[0]()
    inc[cap : 2 * cap] = slot_sum[cap : 2 * cap]
    f_pass(1)
    z_pass(2)
    z_start(3)
    blocks(n_m // 4, n_m // 2, mesh_block)
    p_pass(1)
    blocks(n_m // 2, n_m, mesh_block)
    f_pass(2)
    d_wait(1)
    slot_x[1]()
    names = (1, 2, 3)
    arrived = dot(outer(land), inc[...])
    new = update(outer(mesh), arrived, 1, names, enc_nb, enc_gain)
    framed_a[HALO : 2 * HALO] = new[:HALO]
    framed_a[rows_m : HALO + rows_m] = new[HALO:]
    rims[0][0]()
    z_pass(3)
    p_pass(2)
    arrived = dot(inner(land), inc[...])
    framed_a[2 * HALO : rows_m] = update(inner(mesh), arrived, 1, names, enc_nb, enc_gain)
    blocks(0, n_d, m2g_block)
    f_pass(3)
    d_wait(2)
    w_in = weight(2, 4)
    own = framed_a[HALO : HALO + rows_m]
    ext = framed_a.shape[0]
    terms[HALO : HALO + rows_m] = dot(own, w_in[:width]).astype(BF16)
    terms[ext:] = (dot(own, w_in[width:]) + proc_b1[...]).astype(BF16)
    rims[0][1]()
    rim = jnp.concatenate([framed_a[0:HALO], framed_a[HALO + rows_m :]], axis=0)
    rim_terms = dot(rim, w_in[:width]).astype(BF16)
    terms[0:HALO] = rim_terms[:HALO]
    terms[HALO + rows_m : ext] = rim_terms[HALO:]
    messages(oh_m, terms, oh_m.shape[0])
    p_pass(3)
    names = (5, 6, 7)
    count = oh_m.shape[0]
    arrived = dot(outer(oht_m), msg[0:count])
    new = update(outer(framed_a, HALO), arrived, 2, names, proc_nb, proc_gain)
    framed_b[HALO : 2 * HALO] = new[:HALO]
    framed_b[rows_m : HALO + rows_m] = new[HALO:]
    rims[1][0]()
    arrived = dot(inner(oht_m), msg[0:count])
    framed_b[2 * HALO : rows_m] = update(
        inner(framed_a, HALO), arrived, 2, names, proc_nb, proc_gain
    )
    d_wait(3)
    w_in = weight(3, 8)
    terms_d[ext:] = (dot(grid[...], w_in[width:]) + dec_b1[...]).astype(BF16)
    terms_d[HALO : HALO + rows_m] = dot(framed_b[HALO : HALO + rows_m], w_in[:width]).astype(BF16)
    rims[1][1]()
    rim = jnp.concatenate([framed_b[0:HALO], framed_b[HALO + rows_m :]], axis=0)
    rim_terms = dot(rim, w_in[:width]).astype(BF16)
    terms_d[0:HALO] = rim_terms[:HALO]
    terms_d[HALO + rows_m : ext] = rim_terms[HALO:]
    messages(oh_d, terms_d, oh_d.shape[0])
    names = (9, 10, 11)
    count = oh_d.shape[0]
    middle = grid.shape[0] // 2
    for lo in (0, middle):
        part = slice(lo, lo + middle)
        arrived = dot(oht_d[part], msg[0:count])
        out_ref[part] = update(grid[part], arrived, 3, names, dec_nb, dec_gain)
    for g in range(4):
        finish(g)
    for moves in (slot_x, *rims):
        moves[2]()


def on_device(
    dims,
    grid_state, mesh_state, g2m_sender, g2m_slot, g2m_land,
    mesh_sender, mesh_receiver, m2g_sender, m2g_receiver,
    enc_msg_w1, enc_msg_b1, enc_msg_w2, enc_node_w1, enc_node_b1, enc_node_w2, enc_gain,
    proc_msg_w1, proc_msg_b1, proc_msg_w2, proc_node_w1, proc_node_b1, proc_node_w2, proc_gain,
    dec_msg_w1, dec_msg_b1, dec_msg_w2, dec_node_w1, dec_node_b1, dec_node_w2, dec_gain,
):
    bands = dims[0]
    weights = (
        enc_msg_w1, enc_msg_w2, enc_node_w1, enc_node_w2,
        proc_msg_w1[0], proc_msg_w2[0], proc_node_w1[0], proc_node_w2[0],
        dec_msg_w1, dec_msg_w2, dec_node_w1, dec_node_w2,
    )
    width = grid_state.shape[1]
    rows_g, rows_m = grid_state.shape[0], mesh_state.shape[0]
    slots = g2m_land.shape[0]
    ext = rows_m + 2 * HALO
    plan = {}
    buffers = []
    for members in GROUPS:
        off = 0
        for m in members:
            rows = weights[m].shape[0]
            plan[m] = (off, rows)
            off += rows
        buffers.append(pltpu.VMEM((bands, -(-off // 64) * 64, width), BF16))
    groups = len(GROUPS)
    e_g, e_m, e_d = g2m_sender.shape[0], mesh_sender.shape[0], m2g_sender.shape[0]
    dma = pltpu.SemaphoreType.DMA
    scratch = buffers + [
        pltpu.VMEM((rows_g, width), BF16),
        pltpu.VMEM((rows_m, width), BF16),
        pltpu.VMEM((slots, width), BF16),
        pltpu.VMEM((2 * slots // 3, width), BF16),
        pltpu.VMEM((ext, width), BF16),
        pltpu.VMEM((ext, width), BF16),
        pltpu.VMEM((slots, rows_g), BF16),
        pltpu.VMEM((e_g, rows_g), BF16),
        pltpu.VMEM((slots, e_g), BF16),
        pltpu.VMEM((rows_m, slots), BF16),
        pltpu.VMEM((e_m, ext + rows_m), BF16),
        pltpu.VMEM((rows_m, e_m), BF16),
        pltpu.VMEM((e_d, ext + rows_g), BF16),
        pltpu.VMEM((rows_g, e_d), BF16),
        pltpu.VMEM((ext + rows_m, width), BF16),
        pltpu.VMEM((ext + rows_g, width), BF16),
        pltpu.VMEM((max(e_m, e_d), width), BF16),
        dma((groups, bands)),
        dma((groups, bands)),
        dma((groups, bands, 3)),
        dma((groups, bands, 3)),
        dma((groups, bands, 2)),
        dma((groups, bands, 2)),
        dma((groups, bands)),
        dma((groups, bands)),
        dma((12,)),
        dma((2,)),
        dma((16,)),
        dma((3, 2)),
        dma((3, 2)),
    ]
    table = lambda v: v.reshape(-1, LANES)
    row = lambda v: v.reshape(1, -1)
    small = (
        table(g2m_sender), table(g2m_slot), g2m_land,
        table(mesh_sender), table(mesh_receiver), table(m2g_sender), table(m2g_receiver),
        row(enc_msg_b1), row(enc_node_b1), row(enc_gain),
        proc_msg_b1, proc_node_b1, proc_gain,
        row(dec_msg_b1), row(dec_node_b1), row(dec_gain),
    )
    scratch += [pltpu.VMEM(v.shape, v.dtype) for v in small]
    hbm = pl.BlockSpec(memory_space=pltpu.HBM)
    vmem = pl.BlockSpec(memory_space=pltpu.VMEM)
    return pl.pallas_call(
        functools.partial(kernel, dims, plan),
        out_shape=jax.ShapeDtypeStruct((rows_g, width), BF16),
        in_specs=[hbm] * 30,
        out_specs=vmem,
        scratch_shapes=scratch,
        compiler_params=pltpu.CompilerParams(
            collective_id=0, has_side_effects=True, vmem_limit_bytes=VMEM_LIMIT
        ),
    )(
        grid_state, mesh_state, *small, *weights
    )


def solution(mesh):
    rows = P(("ens", "band", "feat", "sub"), None)
    edges = P(("band", "feat", "sub"))
    flat = P("band", None)
    deep = P(None, "band", None)
    enc = (flat, P(), flat, flat, P(), flat, P())
    proc = (deep, P(), deep, deep, P(), deep, P())
    in_specs = (rows, rows) + (edges,) * 7 + enc + proc + enc
    dims = (mesh.shape["band"], mesh.shape["feat"], mesh.shape["sub"])
    return jax.shard_map(
        functools.partial(on_device, dims),
        mesh=mesh, in_specs=in_specs, out_specs=rows, check_vma=False,
    )
```

```python
import functools

import jax
import jax.numpy as jnp
from jax import lax
from jax.experimental import pallas as pl
from jax.experimental.pallas import tpu as pltpu
from jax.sharding import PartitionSpec as P

HALO = 128
LANES = 128
VMEM_LIMIT = 60 * 1024 * 1024
F32 = jnp.float32
BF16 = jnp.bfloat16
MESH = pl.DeviceIdType.MESH

GROUPS = ((0,), (1, 2, 3), (4, 5, 6, 7), (8, 9, 10, 11))


DIRECT = (0,)


def silu(v):
    h = 0.5 * v
    return h + h * jnp.tanh(h)


def dot(a, b):
    return jnp.dot(a, b, preferred_element_type=F32)


def kernel(dims, plan, *refs):
    bands, feats, subs = dims
    grid_hbm, mesh_hbm = refs[:2]
    small_hbm = refs[2:18]
    shards = refs[18:30]
    out_ref = refs[30]
    (
        w0, w1, w2, w3, grid, mesh, inc, slots_out, framed_a, framed_b, counts,
        oh_g, oht_q, land, oh_m, oht_m, oh_d, oht_d, terms, terms_d, msg,
        zsend, zrecv, psend, precv, fsend, frecv, dsend, drecv,
        wsem, ssem, nsem, hsend, hrecv,
    ) = refs[31:-16]
    (
        g2m_s, g2m_q, g2m_l, mesh_s, mesh_r, m2g_s, m2g_r,
        enc_b1, enc_nb, enc_gain, proc_b1, proc_nb, proc_gain, dec_b1, dec_nb, dec_gain,
    ) = refs[-16:]
    wbufs = (w0, w1, w2, w3)
    y = lax.axis_index("ens")
    z = lax.axis_index("band")
    x = lax.axis_index("feat")
    c = lax.axis_index("sub")
    xn = x + 1 - 2 * lax.rem(x, 2)
    yn = 1 - y
    q = 2 * y + lax.rem(x, 2)
    position = (z * feats + x) * subs + c
    last = bands * feats * subs - 1
    has_left = position > 0
    has_right = position < last

    def place(number):
        return (y, number // (feats * subs), lax.rem(number // subs, feats), lax.rem(number, subs))

    left = place(lax.rem(position + last, last + 1))
    right = place(lax.rem(position + 1, last + 1))
    sibling = (y, z, x, 1 - c)
    peers = ((y, z, xn, c), (yn, z, x, c), (yn, z, xn, c))
    chunks = (2 * y + lax.rem(xn, 2), 2 * yn + lax.rem(x, 2), 2 * yn + lax.rem(xn, 2))

    local = []
    for g, members in enumerate(GROUPS):
        group = []
        for m in members:
            off, rows = plan[m]
            group.append(
                pltpu.make_async_copy(
                    shards[m], wbufs[g].at[z, pl.ds(off, rows), :], wsem.at[m]
                )
            )
        local.append(group)
    states = (
        pltpu.make_async_copy(grid_hbm, grid, ssem.at[0]),
        pltpu.make_async_copy(mesh_hbm, mesh, ssem.at[1]),
    )
    for group in local:
        for copy in group:
            copy.start()
    small = [
        pltpu.make_async_copy(src, dst, nsem.at[i])
        for i, (src, dst) in enumerate(zip(small_hbm, refs[-16:]))
    ]
    for copy in small:
        copy.start()
    for copy in states:
        copy.start()

    barrier = pltpu.get_barrier_semaphore()

    def greet(r, carry):
        pl.semaphore_signal(
            barrier, inc=1, device_id=(y, lax.rem(z + r, bands), x, c), device_id_type=MESH
        )
        return carry

    lax.fori_loop(1, bands, greet, 0)
    for peer in peers:
        pl.semaphore_signal(barrier, inc=1, device_id=peer, device_id_type=MESH)
    for peer in (sibling, left, right):
        pl.semaphore_signal(barrier, inc=1, device_id=peer, device_id_type=MESH)
    pl.semaphore_wait(barrier, bands - 1 + 6)

    def half_rows(g, core):
        half = wbufs[g].shape[1] // 2
        return pl.ds(pl.multiple_of(core * half, 16), half)

    def cols(chunk):
        width = wbufs[0].shape[2] // 4
        return pl.ds(pl.multiple_of(chunk * width, LANES), width)

    def z_copy(g, r, owner, target):
        piece = wbufs[g].at[owner, half_rows(g, c), cols(q)]
        return pltpu.make_async_remote_copy(
            piece, piece, zsend.at[g, r], zrecv.at[g, r],
            device_id=(y, target, x, c), device_id_type=MESH,
        )

    def p_copy(g, r, owner, j, chunk):
        piece = wbufs[g].at[owner, half_rows(g, c), cols(chunk)]
        return pltpu.make_async_remote_copy(
            piece, piece, psend.at[g, r, j], precv.at[g, r, j],
            device_id=peers[j], device_id_type=MESH,
        )

    def d_copy(g, r, owner, core):
        piece = wbufs[g].at[owner, half_rows(g, core), :]
        return pltpu.make_async_remote_copy(
            piece, piece, dsend.at[g, r], drecv.at[g, r],
            device_id=sibling, device_id_type=MESH,
        )

    def each(body):
        def step(r, carry):
            body(r, lax.rem(z - r + bands, bands))
            return carry

        lax.fori_loop(1, bands, step, 0)

    def z_start(g):
        for copy in local[g]:
            copy.wait()
        each(lambda r, owner: z_copy(g, r, z, lax.rem(z + r, bands)).start())

    def direct(g):
        return g in DIRECT

    def f_copy(g, r, owner, i, chunk):
        quarter = wbufs[g].shape[1] // 4
        start = pl.multiple_of((2 * c + i) * quarter, 16)
        piece = wbufs[g].at[owner, pl.ds(start, quarter), cols(chunk)]
        return pltpu.make_async_remote_copy(
            piece, piece, fsend.at[g, r, i], frecv.at[g, r, i],
            device_id=peers[1 - i], device_id_type=MESH,
        )

    def z_pass(g):
        def body(r, owner):
            z_copy(g, r, owner, owner).wait_recv()
            for j in range(3 if direct(g) else 2):
                p_copy(g, r, owner, j, q).start()

        each(body)

    def f_pass(g):
        def body(r, owner):
            for i in range(2):
                p_copy(g, r, owner, i, chunks[i]).wait_recv()
                f_copy(g, r, owner, i, chunks[i]).start()

        each(body)

    def p_pass(g):
        def body(r, owner):
            if direct(g):
                for j in range(3):
                    p_copy(g, r, owner, j, chunks[j]).wait_recv()
            else:
                for i in range(2):
                    f_copy(g, r, owner, i, chunks[2]).wait_recv()
            d_copy(g, r, owner, c).start()

        each(body)

    def d_wait(g):
        each(lambda r, owner: d_copy(g, r, owner, 1 - c).wait_recv())

    def finish(g):
        def body(r, owner):
            z_copy(g, r, z, lax.rem(z + r, bands)).wait_send()
            for j in range(3 if direct(g) else 2):
                p_copy(g, r, owner, j, q).wait_send()
            if not direct(g):
                for i in range(2):
                    f_copy(g, r, owner, i, chunks[i]).wait_send()
            d_copy(g, r, owner, c).wait_send()

        each(body)

    def weight(g, m, first=0, count=None):
        off, rows = plan[m]
        whole = wbufs[g][:, off : off + rows, :]
        return whole.reshape(bands * rows, whole.shape[2])

    def exchange(step, to_left, from_right, to_right, from_left):
        def left_copy():
            return pltpu.make_async_remote_copy(
                to_left, from_right, hsend.at[step, 0], hrecv.at[step, 0],
                device_id=left, device_id_type=MESH,
            )

        def right_copy():
            return pltpu.make_async_remote_copy(
                to_right, from_left, hsend.at[step, 1], hrecv.at[step, 1],
                device_id=right, device_id_type=MESH,
            )

        def start():
            @pl.when(has_left)
            def _():
                left_copy().start()

            @pl.when(has_right)
            def _():
                right_copy().start()

        def wait():
            @pl.when(has_right)
            def _():
                left_copy().wait_recv()

            @pl.when(has_left)
            def _():
                right_copy().wait_recv()

        def done():
            @pl.when(has_left)
            def _():
                left_copy().wait_send()

            @pl.when(has_right)
            def _():
                right_copy().wait_send()

        return start, wait, done

    cap = inc.shape[0] // 3
    rows_m = mesh.shape[0]
    width = mesh.shape[1]
    slot_x = exchange(
        0, slots_out.at[pl.ds(0, cap)], inc.at[pl.ds(0, cap)],
        slots_out.at[pl.ds(cap, cap)], inc.at[pl.ds(2 * cap, cap)],
    )
    rims = tuple(
        exchange(
            1 + i, buf.at[pl.ds(HALO, HALO)], buf.at[pl.ds(HALO + rows_m, HALO)],
            buf.at[pl.ds(rows_m, HALO)], buf.at[pl.ds(0, HALO)],
        )
        for i, buf in enumerate((framed_a, framed_b))
    )

    @pl.when(jnp.logical_not(has_left))
    def _():
        inc[2 * cap : 3 * cap] = jnp.zeros((cap, width), BF16)
        framed_a[0:HALO] = jnp.zeros((HALO, width), BF16)
        framed_b[0:HALO] = jnp.zeros((HALO, width), BF16)

    @pl.when(jnp.logical_not(has_right))
    def _():
        inc[0:cap] = jnp.zeros((cap, width), BF16)
        framed_a[HALO + rows_m :] = jnp.zeros((HALO, width), BF16)
        framed_b[HALO + rows_m :] = jnp.zeros((HALO, width), BF16)

    def pick_rows(target, base, row, first, count):
        column = jnp.broadcast_to(row.astype(F32), (LANES, LANES)).T
        for j in range(count // LANES):
            lane = lax.broadcasted_iota(jnp.int32, (LANES, LANES), 1) + j * LANES
            target[pl.ds(base, LANES), first + j * LANES : first + (j + 1) * LANES] = jnp.where(
                column == lane.astype(F32), 1.0, 0.0
            ).astype(BF16)

    def pick_cols(target, base, row, count):
        sub = lax.broadcasted_iota(jnp.int32, (count, LANES), 0)
        target[:, pl.ds(base, LANES)] = jnp.where(
            sub == jnp.broadcast_to(row, (count, LANES)), 1.0, 0.0
        ).astype(BF16)

    def blocks(first, count, body):
        def step(e, carry):
            body(e, pl.multiple_of(e * LANES, LANES))
            return carry

        lax.fori_loop(first, count, step, 0)

    def g2m_block(e, base):
        pick_rows(oh_g, base, g2m_s[pl.ds(e, 1), :], 0, oh_g.shape[1])
        pick_cols(oht_q, base, g2m_q[pl.ds(e, 1), :], oht_q.shape[0])

    def mesh_block(e, base):
        row = mesh_r[pl.ds(e, 1), :]
        pick_rows(oh_m, base, mesh_s[pl.ds(e, 1), :], 0, framed_a.shape[0])
        pick_rows(oh_m, base, row, framed_a.shape[0], rows_m)
        pick_cols(oht_m, base, row, rows_m)

    def m2g_block(e, base):
        row = m2g_r[pl.ds(e, 1), :]
        pick_rows(oh_d, base, m2g_s[pl.ds(e, 1), :], 0, framed_a.shape[0])
        pick_rows(oh_d, base, row, framed_a.shape[0], grid.shape[0])
        pick_cols(oht_d, base, row, grid.shape[0])

    def update(v, a, g, names, bias, gain_row):
        message_out, node_in, node_out = (weight(g, m) for m in names)
        incoming = dot(a.astype(BF16), message_out).astype(BF16)
        before = dot(v, node_in[:width]) + dot(incoming, node_in[width:]) + bias[...]
        mixed = dot(silu(before).astype(BF16), node_out)
        centred = mixed - jnp.mean(mixed, axis=1, keepdims=True)
        spread = jnp.mean(centred * centred, axis=1, keepdims=True)
        return (v.astype(F32) + centred * lax.rsqrt(spread + 1e-05) * gain_row[...]).astype(BF16)

    def outer(ref, base=0):
        return jnp.concatenate(
            [ref[base : base + HALO], ref[base + rows_m - HALO : base + rows_m]], axis=0
        )

    def inner(ref, base=0):
        return ref[base + HALO : base + rows_m - HALO]

    def messages(oh, table, count):
        size = 256

        def step(e, carry):
            base = pl.multiple_of(e * size, size)
            msg[pl.ds(base, size), :] = silu(dot(oh[pl.ds(base, size), :], table[...])).astype(BF16)
            return carry

        lax.fori_loop(0, count // size, step, 0)

    z_start(0)
    z_start(1)
    for copy in small:
        copy.wait()
    blocks(0, g2m_s.shape[0], g2m_block)
    z_pass(0)
    z_start(2)
    counts[...] = dot(oht_q[...], oh_g[...]).astype(BF16)
    for k in range(3):
        pick_cols(land, k * LANES, g2m_l[k * LANES : (k + 1) * LANES].reshape(1, LANES), rows_m)
    p_pass(0)
    z_pass(1)
    n_m, n_d = mesh_s.shape[0], m2g_s.shape[0]
    blocks(0, n_m // 4, mesh_block)
    for copy in states:
        copy.wait()
    d_wait(0)
    hidden = silu(dot(grid[...], weight(0, 0)) + enc_b1[...]).astype(BF16)
    slot_sum = dot(counts[...], hidden).astype(BF16)
    slots_out[0:cap] = slot_sum[0:cap]
    slots_out[cap : 2 * cap] = slot_sum[2 * cap : 3 * cap]
    slot_x[0]()
    inc[cap : 2 * cap] = slot_sum[cap : 2 * cap]
    f_pass(1)
    z_pass(2)
    z_start(3)
    blocks(n_m // 4, n_m // 2, mesh_block)
    p_pass(1)
    blocks(n_m // 2, n_m, mesh_block)
    f_pass(2)
    blocks(0, n_d, m2g_block)
    d_wait(1)
    slot_x[1]()
    names = (1, 2, 3)
    arrived = dot(outer(land), inc[...])
    new = update(outer(mesh), arrived, 1, names, enc_nb, enc_gain)
    framed_a[HALO : 2 * HALO] = new[:HALO]
    framed_a[rows_m : HALO + rows_m] = new[HALO:]
    rims[0][0]()
    z_pass(3)
    p_pass(2)
    arrived = dot(inner(land), inc[...])
    framed_a[2 * HALO : rows_m] = update(inner(mesh), arrived, 1, names, enc_nb, enc_gain)
    f_pass(3)
    d_wait(2)
    w_in = weight(2, 4)
    own = framed_a[HALO : HALO + rows_m]
    ext = framed_a.shape[0]
    terms[HALO : HALO + rows_m] = dot(own, w_in[:width]).astype(BF16)
    terms[ext:] = (dot(own, w_in[width:]) + proc_b1[...]).astype(BF16)
    rims[0][1]()
    rim = jnp.concatenate([framed_a[0:HALO], framed_a[HALO + rows_m :]], axis=0)
    rim_terms = dot(rim, w_in[:width]).astype(BF16)
    terms[0:HALO] = rim_terms[:HALO]
    terms[HALO + rows_m : ext] = rim_terms[HALO:]
    messages(oh_m, terms, oh_m.shape[0])
    p_pass(3)
    names = (5, 6, 7)
    count = oh_m.shape[0]
    arrived = dot(outer(oht_m), msg[0:count])
    new = update(outer(framed_a, HALO), arrived, 2, names, proc_nb, proc_gain)
    framed_b[HALO : 2 * HALO] = new[:HALO]
    framed_b[rows_m : HALO + rows_m] = new[HALO:]
    rims[1][0]()
    arrived = dot(inner(oht_m), msg[0:count])
    framed_b[2 * HALO : rows_m] = update(
        inner(framed_a, HALO), arrived, 2, names, proc_nb, proc_gain
    )
    d_wait(3)
    w_in = weight(3, 8)
    terms_d[ext:] = (dot(grid[...], w_in[width:]) + dec_b1[...]).astype(BF16)
    terms_d[HALO : HALO + rows_m] = dot(framed_b[HALO : HALO + rows_m], w_in[:width]).astype(BF16)
    rims[1][1]()
    rim = jnp.concatenate([framed_b[0:HALO], framed_b[HALO + rows_m :]], axis=0)
    rim_terms = dot(rim, w_in[:width]).astype(BF16)
    terms_d[0:HALO] = rim_terms[:HALO]
    terms_d[HALO + rows_m : ext] = rim_terms[HALO:]
    messages(oh_d, terms_d, oh_d.shape[0])
    names = (9, 10, 11)
    count = oh_d.shape[0]
    middle = grid.shape[0] // 2
    for lo in (0, middle):
        part = slice(lo, lo + middle)
        arrived = dot(oht_d[part], msg[0:count])
        out_ref[part] = update(grid[part], arrived, 3, names, dec_nb, dec_gain)
    for g in range(4):
        finish(g)
    for moves in (slot_x, *rims):
        moves[2]()


def on_device(
    dims,
    grid_state, mesh_state, g2m_sender, g2m_slot, g2m_land,
    mesh_sender, mesh_receiver, m2g_sender, m2g_receiver,
    enc_msg_w1, enc_msg_b1, enc_msg_w2, enc_node_w1, enc_node_b1, enc_node_w2, enc_gain,
    proc_msg_w1, proc_msg_b1, proc_msg_w2, proc_node_w1, proc_node_b1, proc_node_w2, proc_gain,
    dec_msg_w1, dec_msg_b1, dec_msg_w2, dec_node_w1, dec_node_b1, dec_node_w2, dec_gain,
):
    bands = dims[0]
    weights = (
        enc_msg_w1, enc_msg_w2, enc_node_w1, enc_node_w2,
        proc_msg_w1[0], proc_msg_w2[0], proc_node_w1[0], proc_node_w2[0],
        dec_msg_w1, dec_msg_w2, dec_node_w1, dec_node_w2,
    )
    width = grid_state.shape[1]
    rows_g, rows_m = grid_state.shape[0], mesh_state.shape[0]
    slots = g2m_land.shape[0]
    ext = rows_m + 2 * HALO
    plan = {}
    buffers = []
    for members in GROUPS:
        off = 0
        for m in members:
            rows = weights[m].shape[0]
            plan[m] = (off, rows)
            off += rows
        buffers.append(pltpu.VMEM((bands, -(-off // 64) * 64, width), BF16))
    groups = len(GROUPS)
    e_g, e_m, e_d = g2m_sender.shape[0], mesh_sender.shape[0], m2g_sender.shape[0]
    dma = pltpu.SemaphoreType.DMA
    scratch = buffers + [
        pltpu.VMEM((rows_g, width), BF16),
        pltpu.VMEM((rows_m, width), BF16),
        pltpu.VMEM((slots, width), BF16),
        pltpu.VMEM((2 * slots // 3, width), BF16),
        pltpu.VMEM((ext, width), BF16),
        pltpu.VMEM((ext, width), BF16),
        pltpu.VMEM((slots, rows_g), BF16),
        pltpu.VMEM((e_g, rows_g), BF16),
        pltpu.VMEM((slots, e_g), BF16),
        pltpu.VMEM((rows_m, slots), BF16),
        pltpu.VMEM((e_m, ext + rows_m), BF16),
        pltpu.VMEM((rows_m, e_m), BF16),
        pltpu.VMEM((e_d, ext + rows_g), BF16),
        pltpu.VMEM((rows_g, e_d), BF16),
        pltpu.VMEM((ext + rows_m, width), BF16),
        pltpu.VMEM((ext + rows_g, width), BF16),
        pltpu.VMEM((max(e_m, e_d), width), BF16),
        dma((groups, bands)),
        dma((groups, bands)),
        dma((groups, bands, 3)),
        dma((groups, bands, 3)),
        dma((groups, bands, 2)),
        dma((groups, bands, 2)),
        dma((groups, bands)),
        dma((groups, bands)),
        dma((12,)),
        dma((2,)),
        dma((16,)),
        dma((3, 2)),
        dma((3, 2)),
    ]
    table = lambda v: v.reshape(-1, LANES)
    row = lambda v: v.reshape(1, -1)
    small = (
        table(g2m_sender), table(g2m_slot), g2m_land,
        table(mesh_sender), table(mesh_receiver), table(m2g_sender), table(m2g_receiver),
        row(enc_msg_b1), row(enc_node_b1), row(enc_gain),
        proc_msg_b1, proc_node_b1, proc_gain,
        row(dec_msg_b1), row(dec_node_b1), row(dec_gain),
    )
    scratch += [pltpu.VMEM(v.shape, v.dtype) for v in small]
    hbm = pl.BlockSpec(memory_space=pltpu.HBM)
    vmem = pl.BlockSpec(memory_space=pltpu.VMEM)
    return pl.pallas_call(
        functools.partial(kernel, dims, plan),
        out_shape=jax.ShapeDtypeStruct((rows_g, width), BF16),
        in_specs=[hbm] * 30,
        out_specs=vmem,
        scratch_shapes=scratch,
        compiler_params=pltpu.CompilerParams(
            collective_id=0, has_side_effects=True, vmem_limit_bytes=VMEM_LIMIT
        ),
    )(
        grid_state, mesh_state, *small, *weights
    )


def solution(mesh):
    rows = P(("ens", "band", "feat", "sub"), None)
    edges = P(("band", "feat", "sub"))
    flat = P("band", None)
    deep = P(None, "band", None)
    enc = (flat, P(), flat, flat, P(), flat, P())
    proc = (deep, P(), deep, deep, P(), deep, P())
    in_specs = (rows, rows) + (edges,) * 7 + enc + proc + enc
    dims = (mesh.shape["band"], mesh.shape["feat"], mesh.shape["sub"])
    return jax.shard_map(
        functools.partial(on_device, dims),
        mesh=mesh, in_specs=in_specs, out_specs=rows, check_vma=False,
    )
```
